32 devices in a mesh: gr: 4 (over y, core), gc: 8 (over z, x).
Axes of the slice: x: 2, y: 2, z: 4, core: 2. Of those that a mesh axis runs over, the one named last changes fastest.
Arguments:
- below_factor: bfloat16 [31, 4, 64, 2, 8, 128], P(None, 'gr', None, None, 'gc'), may hold values from -0.0625 to 0.0625
- panel_factor: bfloat16 [31, 4, 64, 512], P(None, 'gr', 'gc'), may hold values from -0.0625 to 0.0625
- prior_factor: bfloat16 [512, 2, 8, 128], P('gr', None, 'gc'), may hold values from -0.25 to 0.25
- diag_factor: float32 [512, 512], replicated, may hold values from -1 to 3, as said below
- diag_inverse: float32 [512, 512], replicated, may hold values from -2 to 1, as said below
- below_adjoint: bfloat16 [31, 4, 64, 2, 8, 128], P(None, 'gr', None, None, 'gc'), may hold values from -6 to 6
- panel_adjoint: bfloat16 [31, 4, 64, 512], P(None, 'gr', 'gc'), may hold values from -6 to 6
- prior_adjoint: bfloat16 [512, 2, 8, 128], P('gr', None, 'gc'), may hold values from -6 to 6
- diag_adjoint: float32 [512, 512], replicated, may hold values from -6 to 6
Outputs:
- below_update: bfloat16 [31, 4, 64, 2, 8, 128], P(None, 'gr', None, None, 'gc')
- panel_gradient: bfloat16 [31, 4, 64, 512], P(None, 'gr', 'gc')
- prior_update: bfloat16 [512, 2, 8, 128], P('gr', None, 'gc')
- diag_gradient: float32 [512, 512], replicated
The draws below stay inside these ranges and needn't reach their ends.
Inputs may be any that keep to these rules, and one draw needn't show every extreme that they name: `diag_factor`: lower triangular, diagonal entries positive. `diag_inverse`: the inverse of diag_factor.
All inputs are finite; a program needn't handle non-finite values.
Results may differ from the reference program's by a relative error of at most 0.015.
Values may be sent and summed in bfloat16 or wider, within the bound.
No kernel may reach another device: no remote copies, remote signals or barrier semaphores. Data moves between devices by JAX's collectives and lax.ppermute only.
A program may use at most 64 MiB of HBM per device.

```python
import math
import jax
import jax.numpy as jnp
from jax import lax

NB = 512
RB = 64
CB = 128
RT = 31
CT = 2
MB = 7936
PRIOR = 2048
N_GR = 4
N_GC = 8


def lower_factor(key):
    inner_key = jax.random.fold_in(key, 7)
    diag_key, off_key = jax.random.split(inner_key)
    diagonal = jax.random.uniform(diag_key, (NB,), jnp.float32, 1.0, 2.0)
    offdiag = jax.random.normal(off_key, (NB, NB), jnp.float32) * (0.5 / math.sqrt(NB))
    return jnp.tril(offdiag, -1) + jnp.diag(diagonal)


def draw_diag_factor(key, part):
    return lower_factor(key)


def draw_diag_inverse(key, part):
    factor = lower_factor(key)
    return jax.scipy.linalg.solve_triangular(factor, jnp.eye(NB, dtype=jnp.float32), lower=True)


def levels(stream_key, dims, shards, low, largest):
    def one(position, blocks):
        draws = jax.random.uniform(jax.random.fold_in(jax.random.fold_in(stream_key, 6), position), (blocks,), jnp.float32, low / len(shards), largest / len(shards))
        return jnp.repeat(jnp.exp(draws), dims[position] // blocks).reshape((-1,) + (1,) * (len(dims) - position - 1))

    level = one(*shards[0])
    for cut in shards[1:]:
        level = level * one(*cut)
    return level


def noise(stream_key, extent, deviation, reach, cuts=(), kind=jnp.bfloat16):
    entries = deviation * jax.random.normal(stream_key, extent, jnp.float32)
    if cuts:
        entries = entries * levels(stream_key, extent, cuts, -0.22, 0.18)
    return jnp.clip(entries, -reach, reach).astype(kind)


def setup_inputs(seed: int = 0) -> dict:
    arg_keys = jax.random.split(jax.random.key(seed), 10)
    below_factor = noise(arg_keys[0], (RT, N_GR, RB, CT, N_GC, CB), MB ** -0.5, 0.0625, ((1, 4), (4, 8)))
    panel_factor = noise(arg_keys[1], (RT, N_GR, RB, NB), MB ** -0.5, 0.0625, ((1, 4), (2, 8)))
    prior_factor = noise(arg_keys[2], (NB, CT, N_GC, CB), NB ** -0.5, 0.25, ((0, 4), (2, 8)))
    diag_factor = draw_diag_factor(jax.random.fold_in(arg_keys[9], 71), 0)
    diag_inverse = draw_diag_inverse(jax.random.fold_in(arg_keys[9], 71), 0)
    below_adjoint = noise(arg_keys[5], (RT, N_GR, RB, CT, N_GC, CB), 1.0, 6.0, ((1, 4), (4, 8)))
    panel_adjoint = noise(arg_keys[6], (RT, N_GR, RB, NB), 1.0, 6.0, ((1, 4), (2, 8)))
    prior_adjoint = noise(arg_keys[7], (NB, CT, N_GC, CB), 1.0, 6.0, ((0, 4), (2, 8)))
    diag_adjoint = noise(arg_keys[8], (NB, NB), 1.0, 6.0, (), jnp.float32)
    return dict(below_factor=below_factor, panel_factor=panel_factor, prior_factor=prior_factor, diag_factor=diag_factor, diag_inverse=diag_inverse, below_adjoint=below_adjoint, panel_adjoint=panel_adjoint, prior_adjoint=prior_adjoint, diag_adjoint=diag_adjoint)


def row_product(left_rows, right_rows):
    return lax.dot_general(left_rows.astype(jnp.float32), right_rows.astype(jnp.float32), (((0,), (0,)), ((), ())), preferred_element_type=jnp.float32)

def diag_solve(diag_factor, diag_inverse, diag_reduced):
    highest = lax.Precision.HIGHEST
    chol_proj = jnp.dot(diag_factor.T, diag_reduced, precision=highest)
    phi_lower = jnp.tril(chol_proj) - 0.5 * jnp.diag(jnp.diagonal(chol_proj))
    symmetric = 0.5 * (phi_lower + phi_lower.T)
    left_side = jnp.dot(diag_inverse.T, symmetric, precision=highest)
    return jnp.dot(left_side, diag_inverse, precision=highest)

def reference(below_factor, panel_factor, prior_factor, diag_factor, diag_inverse, below_adjoint, panel_adjoint, prior_adjoint, diag_adjoint):
    below_mat = below_factor.reshape(MB, PRIOR)
    below_bar = below_adjoint.reshape(MB, PRIOR)
    panel_mat = panel_factor.reshape(MB, NB)
    panel_bar = panel_adjoint.reshape(MB, NB)
    prior_mat = prior_factor.reshape(NB, PRIOR)
    prior_bar = prior_adjoint.reshape(NB, PRIOR)
    inverse_bf = diag_inverse.astype(jnp.bfloat16)
    panel_grad = jnp.dot(panel_bar.astype(jnp.float32), inverse_bf.astype(jnp.float32), preferred_element_type=jnp.float32).astype(jnp.bfloat16)
    cross_diag = row_product(panel_grad, panel_mat)
    diag_reduced = jnp.tril(diag_adjoint - cross_diag)
    diag_gradient = diag_solve(diag_factor, diag_inverse, diag_reduced)
    twice_bf = (2.0 * diag_gradient).astype(jnp.bfloat16)
    below_new = (below_bar.astype(jnp.float32) - jnp.dot(panel_grad.astype(jnp.float32), prior_mat.astype(jnp.float32), preferred_element_type=jnp.float32)).astype(jnp.bfloat16)
    prior_new = (prior_bar.astype(jnp.float32) - row_product(panel_grad, below_mat) - jnp.dot(twice_bf.astype(jnp.float32), prior_mat.astype(jnp.float32), preferred_element_type=jnp.float32)).astype(jnp.bfloat16)
    return (below_new.reshape(below_adjoint.shape), panel_grad.reshape(panel_factor.shape), prior_new.reshape(prior_adjoint.shape), diag_gradient)
```

```python
import functools

import jax
import jax.numpy as jnp
from jax import lax
from jax.experimental import pallas as pl
from jax.experimental.pallas import tpu as pltpu
from jax.sharding import PartitionSpec as P

BF = jnp.bfloat16
F32 = jnp.float32
BLK = 128


def row_product(left_rows, right_rows):
    return lax.dot_general(
        left_rows, right_rows, (((0,), (0,)), ((), ())), preferred_element_type=F32
    )


def diag_solve(diag_factor, diag_inverse, diag_reduced):
    highest = lax.Precision.HIGHEST
    chol_proj = jnp.dot(diag_factor.T, diag_reduced, precision=highest)
    phi_lower = jnp.tril(chol_proj) - 0.5 * jnp.diag(jnp.diagonal(chol_proj))
    symmetric = 0.5 * (phi_lower + phi_lower.T)
    left_side = jnp.dot(diag_inverse.T, symmetric, precision=highest)
    return jnp.dot(left_side, diag_inverse, precision=highest)


def local_any(
    below_factor,
    panel_factor,
    prior_factor,
    diag_factor,
    diag_inverse,
    below_adjoint,
    panel_adjoint,
    prior_adjoint,
    diag_adjoint,
):
    tile_count = below_factor.shape[0]
    tile_rows = below_factor.shape[2]
    local_rows = tile_count * tile_rows
    local_cols = below_factor.shape[3] * below_factor.shape[5]
    own_rows = panel_factor.shape[2]
    width = panel_factor.shape[3]
    prior_local = prior_factor.shape[0]
    below_mat = below_factor.reshape(local_rows, local_cols)
    below_bar = below_adjoint.reshape(local_rows, local_cols)
    inverse_bf = diag_inverse.astype(BF)
    own_grad = jnp.dot(
        panel_adjoint.reshape(tile_count * own_rows, width),
        inverse_bf,
        preferred_element_type=F32,
    ).astype(BF)
    summed = lax.psum(
        row_product(own_grad, panel_factor.reshape(tile_count * own_rows, width)).astype(BF),
        ("gr", "gc"),
    ).astype(F32)
    panel_grad = own_grad.reshape(panel_adjoint.shape)
    grad_rows = lax.all_gather(panel_grad, "gc", axis=2, tiled=True).reshape(local_rows, width)
    diag_reduced = jnp.tril(diag_adjoint - summed)
    diag_gradient = diag_solve(diag_factor, diag_inverse, diag_reduced)
    prior_here = prior_factor.reshape(prior_local, local_cols)
    prior_whole = lax.all_gather(prior_here, "gr", axis=0, tiled=True)
    below_new = (
        below_bar.astype(F32) - jnp.dot(grad_rows, prior_whole, preferred_element_type=F32)
    ).astype(BF)
    crossing = lax.psum_scatter(
        row_product(grad_rows, below_mat).astype(BF), "gr", scatter_dimension=0, tiled=True
    ).astype(F32)
    twice_rows = lax.dynamic_slice_in_dim(
        2.0 * diag_gradient, lax.axis_index("gr") * prior_local, prior_local, 0
    ).astype(BF)
    curvature = jnp.dot(twice_rows, prior_whole, preferred_element_type=F32)
    prior_bar = prior_adjoint.reshape(prior_local, local_cols).astype(F32)
    prior_new = (prior_bar - crossing - curvature).astype(BF)
    return (
        below_new.reshape(below_adjoint.shape),
        panel_grad,
        prior_new.reshape(prior_adjoint.shape),
        diag_gradient,
    )


VM = pl.BlockSpec(memory_space=pltpu.VMEM)


def call(body, outs, ins, scratch=(), flops=0, nbytes=0, name=None):
    return pl.pallas_call(
        body,
        out_shape=[jax.ShapeDtypeStruct(s, d) for s, d in outs],
        in_specs=[VM] * len(ins),
        out_specs=[VM] * len(outs),
        scratch_shapes=list(scratch),
        compiler_params=pltpu.CompilerParams(vmem_limit_bytes=40 * 2**20),
        cost_estimate=pl.CostEstimate(flops=flops, bytes_accessed=nbytes, transcendentals=0),
        name=name,
    )(*ins)


def lower_blocks(count):
    return [(r, c) for r in range(count) for c in range(r + 1)]


def my_core():
    return lax.rem(lax.axis_index("gr"), 2)


def my_y():
    return lax.div(lax.axis_index("gr"), 2)


def grad_kernel(adj, fac, inv, grad, keep, send):
    grad_bf = jnp.dot(adj[...], inv[...].astype(BF), preferred_element_type=F32).astype(BF)
    grad[...] = grad_bf
    blocks = lower_blocks(adj.shape[1] // BLK)
    half = len(blocks) // 2
    core = my_core()
    for row in range(adj.shape[1] // BLK):
        strip = row_product(
            grad_bf[:, row * BLK : (row + 1) * BLK], fac[:, : (row + 1) * BLK]
        )
        for col in range(row + 1):
            at = blocks.index((row, col))
            which, place = at // half, at % half
            piece = strip[:, col * BLK : (col + 1) * BLK]
            here = pl.ds(place * BLK, BLK)

            @pl.when(core == which)
            def _():
                keep[here, :] = piece

            @pl.when(core != which)
            def _():
                send[here, :] = piece.astype(BF)


def split(value):
    high = value.astype(BF)
    return high, (value - high.astype(F32)).astype(BF)


def prep_kernel(fac, inv, fac_t_hi, fac_t_lo, inv_t_hi, inv_t_lo, inv_hi, inv_lo):
    fac_t_hi[...], fac_t_lo[...] = split(fac[...].T)
    inverse = inv[...]
    inv_t_hi[...], inv_t_lo[...] = split(inverse.T)
    inv_hi[...], inv_lo[...] = split(inverse)


def dot3(a_hi, a_lo, b):
    b_hi, b_lo = split(b)
    d = functools.partial(jnp.dot, preferred_element_type=F32)
    return d(a_hi, b_hi) + (d(a_lo, b_hi) + d(a_hi, b_lo))


def dot3r(a, b_hi, b_lo):
    a_hi, a_lo = split(a)
    d = functools.partial(jnp.dot, preferred_element_type=F32)
    return d(a_hi, b_hi) + (d(a_lo, b_hi) + d(a_hi, b_lo))


def natural(view, scratch):
    rows = view.shape[0] // 2
    scratch[...] = view.astype(F32)
    return jnp.concatenate(
        [scratch[pl.ds(t, rows, stride=2), :] for t in range(2)], axis=1
    ).astype(BF)


def place_quarters(refs, store):
    core, y = my_core(), my_y()
    for k, ref in enumerate(refs):
        store(jnp.bitwise_xor(y, k % 2), jnp.bitwise_xor(core, k // 2), ref)


def natural_prior(refs, scratch, whole):
    def put(y, core, ref):
        at = pl.multiple_of((2 * y + core) * BLK, BLK)
        whole[pl.ds(at, BLK), :] = natural(ref[...], scratch)

    place_quarters(refs, put)


def solve_kernel(
    c0, c1, c2, c3, p0, p1, p2, p3, bar, dadj,
    fac_t_hi, fac_t_lo, inv_t_hi, inv_t_lo, inv_hi, inv_lo,
    out, rest, cross, whole, twice, inter,
):
    quarter = c0.shape[0]

    def put(y, core, ref):
        at = pl.multiple_of((2 * core + y) * quarter, quarter)
        cross[pl.ds(at, quarter), :] = ref[...].astype(F32)

    place_quarters((c0, c1, c2, c3), put)
    natural_prior((p0, p1, p2, p3), inter, whole)
    size = dadj.shape[0]
    count = size // BLK
    blocks = lower_blocks(count)
    zero = jnp.zeros((BLK, BLK), F32)
    strips = []
    for row in range(count):
        parts = []
        for col in range(count):
            if col > row:
                parts.append(zero)
            else:
                at = blocks.index((row, col))
                parts.append(
                    dadj[row * BLK : (row + 1) * BLK, col * BLK : (col + 1) * BLK]
                    - cross[at * BLK : (at + 1) * BLK, :]
                )
        strips.append(jnp.concatenate(parts, axis=1))
    reduced = jnp.concatenate(strips, axis=0)
    r_at = lax.broadcasted_iota(jnp.int32, (size, size), 0)
    c_at = lax.broadcasted_iota(jnp.int32, (size, size), 1)
    reduced = jnp.where(r_at >= c_at, reduced, 0.0)
    proj = dot3(fac_t_hi[...], fac_t_lo[...], reduced)
    phi = jnp.where(r_at > c_at, proj, jnp.where(r_at == c_at, 0.5 * proj, 0.0))
    left = dot3(inv_t_hi[...], inv_t_lo[...], phi)
    full = dot3r(left, inv_hi[...], inv_lo[...])
    grad = 0.5 * (full + full.T)
    out[...] = grad
    twice[...] = 2.0 * grad
    own = pl.multiple_of(lax.axis_index("gr") * BLK, BLK)
    rows = twice[pl.ds(own, BLK), :].astype(BF)
    curvature = jnp.dot(rows, whole[...], preferred_element_type=F32)
    inter[...] = bar[...].astype(F32)
    prior_bar = jnp.concatenate(
        [inter[pl.ds(t, BLK, stride=2), :] for t in range(2)], axis=1
    )
    rest[...] = prior_bar - curvature


def final_kernel(rest, keep, recv, out, inter):
    value = rest[...] - (keep[...] + recv[...].astype(F32))
    for t in range(2):
        inter[pl.ds(t, BLK, stride=2), :] = value[:, t * BLK : (t + 1) * BLK]
    out[...] = inter[...].astype(BF)


def ring_order(n):
    return list(range(0, n, 2)) + list(range(n - 1, 0, -2))


def shard_of(offset, n):
    me = lax.axis_index("gc")
    half = lax.div(me, 2)
    pos = jnp.where(lax.rem(me, 2) == 0, half, n - 1 - half)
    at = lax.rem(pos - offset + 2 * n, n)
    return jnp.where(at < n // 2, 2 * at, 2 * (n - 1 - at) + 1)


def crossing_kernel(offsets, n, *refs):
    grads = refs[: len(offsets)]
    below, keep, send, inter, acc = refs[len(offsets) :]
    for k, off in enumerate(offsets):
        j = shard_of(off, n)
        view = below[:, j]
        rows = natural(view.reshape(view.shape[0] * view.shape[1], view.shape[2]), inter)
        part = row_product(grads[k][...], rows)
        if k == 0:
            acc[...] = part
        else:
            acc[...] += part
    core = my_core()
    for which in range(2):
        for y in range(2):
            piece = acc[(2 * y + which) * BLK : (2 * y + which + 1) * BLK, :]

            @pl.when(core == which)
            def _():
                keep[y] = piece

            @pl.when(core != which)
            def _():
                send[y] = piece.astype(BF)


def below_kernel(offsets, n, *refs):
    grads = refs[: len(offsets)]
    p0, p1, p2, p3, bar, out, inter, small, whole = refs[len(offsets) :]
    natural_prior((p0, p1, p2, p3), small, whole)
    for k, off in enumerate(offsets):
        j = shard_of(off, n)
        prod = jnp.dot(grads[k][...], whole[...], preferred_element_type=F32)
        for t in range(2):
            inter[pl.ds(t, prod.shape[0], stride=2), :] = prod[:, t * BLK : (t + 1) * BLK]
        view = bar[:, j]
        old = view.reshape(view.shape[0] * view.shape[1], view.shape[2]).astype(F32)
        out[:, j] = (old - inter[...]).astype(BF).reshape(view.shape)


def xor_perm(n, bit):
    return [(i, i ^ bit) for i in range(n)]


def local_fast(
    below_factor,
    panel_factor,
    prior_factor,
    diag_factor,
    diag_inverse,
    below_adjoint,
    panel_adjoint,
    prior_adjoint,
    diag_adjoint,
    n_gr,
    n_gc,
):
    tiles, _, tile_rows, ct, _, cb = below_factor.shape
    own_rows, width = panel_factor.shape[2:]
    shard_rows = tiles * own_rows
    cols = ct * cb
    prior_local = prior_factor.shape[0]
    core = lambda v: lax.ppermute(v, "gr", xor_perm(n_gr, 1))
    ynb = lambda v: lax.ppermute(v, "gr", xor_perm(n_gr, 2))
    gcx = lambda v, bit: lax.ppermute(v, "gc", xor_perm(n_gc, bit))
    cyc = ring_order(n_gc)
    right = [(cyc[i], cyc[(i + 1) % n_gc]) for i in range(n_gc)]
    left = [(b, a) for a, b in right]

    bf_view = below_factor.reshape(tiles, n_gc, own_rows * ct, cb)
    ba_view = below_adjoint.reshape(tiles, n_gc, own_rows * ct, cb)
    pf_view = prior_factor.reshape(prior_local * ct, cb)
    pa_view = prior_adjoint.reshape(prior_local * ct, cb)

    n_blocks = len(lower_blocks(width // BLK))
    half_rows = n_blocks // 2 * BLK
    quarter = half_rows // 2
    grad, keep, send = call(
        grad_kernel,
        [((shard_rows, width), BF), ((half_rows, BLK), F32), ((half_rows, BLK), BF)],
        [
            panel_adjoint.reshape(shard_rows, width),
            panel_factor.reshape(shard_rows, width),
            diag_inverse,
        ],
        flops=4 * shard_rows * width * width,
        nbytes=2**21,
        name="panel_grad",
    )

    got = core(send)
    y = my_y()
    both = (keep + got.astype(F32)).reshape(2, quarter, BLK)
    mine = lax.dynamic_index_in_dim(both, y, 0, keepdims=False)
    other = lax.dynamic_index_in_dim(both, 1 - y, 0, keepdims=False).astype(BF)
    part = (mine + ynb(other).astype(F32)).astype(BF)
    part = (part.astype(F32) + gcx(part, 1).astype(F32)).astype(BF)
    p2, p4, p6 = gcx(part, 2), gcx(part, 4), gcx(part, 6)
    part = (
        (part.astype(F32) + p2.astype(F32)) + (p4.astype(F32) + p6.astype(F32))
    ).astype(BF)
    part_y = ynb(part)
    part_c = core(part)
    part_b = core(part_y)

    grads, offsets = [grad], [0]
    r = l = grad
    for step in range(1, n_gc // 2 + 1):
        r = lax.ppermute(r, "gc", right)
        grads.append(r)
        offsets.append(step)
        if step < n_gc - step:
            l = lax.ppermute(l, "gc", left)
            grads.append(l)
            offsets.append(-step)

    pf_y = ynb(pf_view)
    pf_c = core(pf_view)
    pf_b = core(pf_y)
    priors = [pf_view, pf_y, pf_c, pf_b]

    prepared = call(
        prep_kernel,
        [((width, width), BF)] * 6,
        [diag_factor, diag_inverse],
        flops=10 * width * width,
        nbytes=2**22,
        name="prep",
    )

    keep_x, send_x = call(
        functools.partial(crossing_kernel, offsets, n_gc),
        [((2, BLK, cols), F32), ((2, BLK, cols), BF)],
        [*grads, bf_view],
        scratch=[
            pltpu.VMEM((shard_rows * ct, cb), F32),
            pltpu.VMEM((width, cols), F32),
        ],
        flops=2 * shard_rows * n_gc * width * cols,
        nbytes=2**22,
        name="crossing",
    )
    both_x = keep_x + core(send_x).astype(F32)
    mine_x = lax.dynamic_index_in_dim(both_x, y, 0, keepdims=False)
    other_x = lax.dynamic_index_in_dim(both_x, 1 - y, 0, keepdims=False).astype(BF)
    got_x = ynb(other_x)

    (below_new,) = call(
        functools.partial(below_kernel, offsets, n_gc),
        [(ba_view.shape, BF)],
        [*grads, *priors, ba_view],
        scratch=[
            pltpu.VMEM((shard_rows * ct, cb), F32),
            pltpu.VMEM((prior_local * ct, cb), F32),
            pltpu.VMEM((width, cols), BF),
        ],
        flops=2 * shard_rows * n_gc * width * cols,
        nbytes=2**22,
        name="below",
    )

    diag_gradient, rest = call(
        solve_kernel,
        [((width, width), F32), ((prior_local, cols), F32)],
        [part, part_y, part_c, part_b, *priors, pa_view, diag_adjoint, *prepared],
        scratch=[
            pltpu.VMEM((n_blocks * BLK, BLK), F32),
            pltpu.VMEM((width, cols), BF),
            pltpu.VMEM((width, width), F32),
            pltpu.VMEM((prior_local * ct, cb), F32),
        ],
        flops=18 * width**3,
        nbytes=2**22,
        name="solve",
    )
    (prior_new,) = call(
        final_kernel,
        [(pa_view.shape, BF)],
        [rest, mine_x, got_x],
        scratch=[pltpu.VMEM((prior_local * ct, cb), F32)],
        flops=10 * prior_local * cols,
        nbytes=2**18,
        name="prior_sum",
    )
    return (
        below_new.reshape(below_adjoint.shape),
        grad.reshape(panel_adjoint.shape),
        prior_new.reshape(prior_adjoint.shape),
        diag_gradient,
    )


def solution(mesh):
    n_gr, n_gc = mesh.shape["gr"], mesh.shape["gc"]

    def local(*args):
        below_factor, panel_factor, prior_factor = args[:3]
        fits = (
            n_gr == 4
            and n_gc == 8
            and panel_factor.shape[2] == 8
            and below_factor.shape[3] == 2
            and below_factor.shape[5] == BLK
            and prior_factor.shape[0] == BLK
        )
        if fits:
            return local_fast(*args, n_gr=n_gr, n_gc=n_gc)
        return local_any(*args)

    in_specs = (
        P(None, "gr", None, None, "gc", None),
        P(None, "gr", "gc", None),
        P("gr", None, "gc", None),
        P(),
        P(),
        P(None, "gr", None, None, "gc", None),
        P(None, "gr", "gc", None),
        P("gr", None, "gc", None),
        P(),
    )
    out_specs = (
        P(None, "gr", None, None, "gc", None),
        P(None, "gr", "gc", None),
        P("gr", None, "gc", None),
        P(),
    )
    return jax.shard_map(local, mesh=mesh, in_specs=in_specs, out_specs=out_specs, check_vma=False)
```

```python
import functools

import jax
import jax.numpy as jnp
from jax import lax
from jax.experimental import pallas as pl
from jax.experimental.pallas import tpu as pltpu
from jax.sharding import PartitionSpec as P

BF = jnp.bfloat16
F32 = jnp.float32
BLK = 128


def row_product(left_rows, right_rows):
    return lax.dot_general(
        left_rows, right_rows, (((0,), (0,)), ((), ())), preferred_element_type=F32
    )


def diag_solve(diag_factor, diag_inverse, diag_reduced):
    highest = lax.Precision.HIGHEST
    chol_proj = jnp.dot(diag_factor.T, diag_reduced, precision=highest)
    phi_lower = jnp.tril(chol_proj) - 0.5 * jnp.diag(jnp.diagonal(chol_proj))
    symmetric = 0.5 * (phi_lower + phi_lower.T)
    left_side = jnp.dot(diag_inverse.T, symmetric, precision=highest)
    return jnp.dot(left_side, diag_inverse, precision=highest)


def local_any(
    below_factor,
    panel_factor,
    prior_factor,
    diag_factor,
    diag_inverse,
    below_adjoint,
    panel_adjoint,
    prior_adjoint,
    diag_adjoint,
):
    tile_count = below_factor.shape[0]
    tile_rows = below_factor.shape[2]
    local_rows = tile_count * tile_rows
    local_cols = below_factor.shape[3] * below_factor.shape[5]
    own_rows = panel_factor.shape[2]
    width = panel_factor.shape[3]
    prior_local = prior_factor.shape[0]
    below_mat = below_factor.reshape(local_rows, local_cols)
    below_bar = below_adjoint.reshape(local_rows, local_cols)
    inverse_bf = diag_inverse.astype(BF)
    own_grad = jnp.dot(
        panel_adjoint.reshape(tile_count * own_rows, width),
        inverse_bf,
        preferred_element_type=F32,
    ).astype(BF)
    summed = lax.psum(
        row_product(own_grad, panel_factor.reshape(tile_count * own_rows, width)).astype(BF),
        ("gr", "gc"),
    ).astype(F32)
    panel_grad = own_grad.reshape(panel_adjoint.shape)
    grad_rows = lax.all_gather(panel_grad, "gc", axis=2, tiled=True).reshape(local_rows, width)
    diag_reduced = jnp.tril(diag_adjoint - summed)
    diag_gradient = diag_solve(diag_factor, diag_inverse, diag_reduced)
    prior_here = prior_factor.reshape(prior_local, local_cols)
    prior_whole = lax.all_gather(prior_here, "gr", axis=0, tiled=True)
    below_new = (
        below_bar.astype(F32) - jnp.dot(grad_rows, prior_whole, preferred_element_type=F32)
    ).astype(BF)
    crossing = lax.psum_scatter(
        row_product(grad_rows, below_mat).astype(BF), "gr", scatter_dimension=0, tiled=True
    ).astype(F32)
    twice_rows = lax.dynamic_slice_in_dim(
        2.0 * diag_gradient, lax.axis_index("gr") * prior_local, prior_local, 0
    ).astype(BF)
    curvature = jnp.dot(twice_rows, prior_whole, preferred_element_type=F32)
    prior_bar = prior_adjoint.reshape(prior_local, local_cols).astype(F32)
    prior_new = (prior_bar - crossing - curvature).astype(BF)
    return (
        below_new.reshape(below_adjoint.shape),
        panel_grad,
        prior_new.reshape(prior_adjoint.shape),
        diag_gradient,
    )


TIES = {'r1': 'sum', 'r2': 'none', 'r3': 'z1sum', 'r4': 'none', 's1': 'z1', 's2': 'z1', 's3': 'z2sum', 's4': 'none', 'pf': 'xsum', 'prep': 'xsum', 'below': 'ag'}
SPLIT, CUT, LATE, LIM = True, 112, False, 40 * 2**20
VM = pl.BlockSpec(memory_space=pltpu.VMEM)
ANYM = pl.BlockSpec(memory_space=pl.ANY)


def call(body, outs, ins, scratch=(), flops=0, nbytes=0, name=None, specs=None,
         out_specs=None, limit=LIM, alias=None):
    return pl.pallas_call(
        body,
        out_shape=[jax.ShapeDtypeStruct(s, d) for s, d in outs],
        in_specs=specs or [VM] * len(ins),
        out_specs=out_specs or [VM] * len(outs),
        scratch_shapes=list(scratch),
        compiler_params=pltpu.CompilerParams(vmem_limit_bytes=limit),
        cost_estimate=pl.CostEstimate(flops=flops, bytes_accessed=nbytes, transcendentals=0),
        name=name,
        input_output_aliases=alias or {},
    )(*ins)


def lower_blocks(count):
    return [(r, c) for r in range(count) for c in range(r + 1)]


def my_core():
    return lax.rem(lax.axis_index("gr"), 2)


def my_y():
    return lax.div(lax.axis_index("gr"), 2)


def grad_kernel(adj, fac, inv, prior, grad, keep, send, adj_v, fac_v, inv_v, grad_v, sems):
    half = keep.shape[0]
    pairs = [(adj, adj_v), (inv, inv_v), (fac, fac_v), (prior, send.at[half:, :])]
    copies = [
        pltpu.make_async_copy(src, dst, sems.at[k]) for k, (src, dst) in enumerate(pairs)
    ]
    for copy in copies:
        copy.start()
    copies[0].wait()
    copies[1].wait()
    grad_v[...] = jnp.dot(
        adj_v[...], inv_v[...].astype(BF), preferred_element_type=F32
    ).astype(BF)
    back = pltpu.make_async_copy(grad_v, grad, sems.at[4])
    back.start()
    copies[2].wait()
    blocks = lower_blocks(adj.shape[1] // BLK)
    core = my_core()
    whole = row_product(grad_v[...], fac_v[...])
    for at, (row, col) in enumerate(blocks):
        which, place = divmod(at * BLK, half)
        piece = whole[row * BLK : (row + 1) * BLK, col * BLK : (col + 1) * BLK]
        here = pl.ds(place, BLK)

        @pl.when(core == which)
        def _():
            keep[here, :] = piece

        @pl.when(core != which)
        def _():
            send[here, :] = piece.astype(BF)

    copies[3].wait()
    back.wait()


def split(value):
    high = value.astype(BF)
    return high, (value - high.astype(F32)).astype(BF)


def prep_kernel(fac, inv, fac_t_hi, fac_t_lo, inv_t_hi, inv_t_lo, inv_hi, inv_lo, done):
    done[...] = jnp.zeros_like(done)
    fac_t_hi[...], fac_t_lo[...] = split(fac[...].T)
    inverse = inv[...]
    inv_t_hi[...], inv_t_lo[...] = split(inverse.T)
    inv_hi[...], inv_lo[...] = split(inverse)


def dot2(a_hi, a_lo, b):
    d = functools.partial(jnp.dot, preferred_element_type=F32)
    return d(a_hi, b) + d(a_lo, b)


def dot2r(a, b_hi, b_lo):
    d = functools.partial(jnp.dot, preferred_element_type=F32)
    return d(a, b_hi) + d(a, b_lo)


def natural(view, scratch):
    rows = view.shape[0] // 2
    scratch[...] = view.astype(F32)
    return jnp.concatenate(
        [scratch[pl.ds(t, rows, stride=2), :] for t in range(2)], axis=1
    ).astype(BF)


def natural_prior(own, other, scratch, whole):
    rows = own.shape[0] // 2
    core, y = my_core(), my_y()
    for ref, where in ((own, y), (other, 1 - y)):
        for k in range(2):
            at = pl.multiple_of((2 * where + jnp.bitwise_xor(core, k)) * BLK, BLK)
            whole[pl.ds(at, BLK), :] = natural(ref[k * rows : (k + 1) * rows, :], scratch)


def solve_kernel(
    c_own, c_y, c_core, prior, bar, dadj,
    fac_t_hi, fac_t_lo, inv_t_hi, inv_t_lo, inv_hi, inv_lo, *others
):
    out, rest, cross, full, twice, inter = others[-6:]
    quarter = c_own.shape[0]
    core, y = my_core(), my_y()
    for where, off, ref in ((core, y, c_own[...]), (core, 1 - y, c_y[...]),
                            (1 - core, y, c_core[:quarter, :]),
                            (1 - core, 1 - y, c_core[quarter:, :])):
        at = pl.multiple_of((2 * where + off) * quarter, quarter)
        cross[pl.ds(at, quarter), :] = ref.astype(F32)
    size = dadj.shape[0]
    half = size // 2
    blocks = lower_blocks(size // BLK)
    top, low = slice(0, half), slice(half, size)
    r_at = lax.broadcasted_iota(jnp.int32, (half, half), 0)
    c_at = lax.broadcasted_iota(jnp.int32, (half, half), 1)

    def reduced(rows, cols):
        strips = []
        for row in range(rows.start // BLK, rows.stop // BLK):
            parts = []
            for col in range(cols.start // BLK, cols.stop // BLK):
                if col > row:
                    parts.append(jnp.zeros((BLK, BLK), F32))
                    continue
                at = blocks.index((row, col))
                here = dadj[row * BLK : (row + 1) * BLK, col * BLK : (col + 1) * BLK]
                parts.append(here - cross[at * BLK : (at + 1) * BLK, :])
            strips.append(jnp.concatenate(parts, axis=1))
        return jnp.concatenate(strips, axis=0)

    def lower(value, scale):
        zero = jnp.zeros_like(value)
        return jnp.where(r_at > c_at, value, jnp.where(r_at == c_at, scale * value, zero))

    d_tt = lower(reduced(top, top), 1.0).astype(BF)
    d_lt = reduced(low, top).astype(BF)
    d_ll = lower(reduced(low, low), 1.0).astype(BF)
    p_tt = dot2(fac_t_hi[top, :], fac_t_lo[top, :], jnp.concatenate([d_tt, d_lt], axis=0))
    p_l = dot2(
        fac_t_hi[low, low], fac_t_lo[low, low], jnp.concatenate([d_lt, d_ll], axis=1)
    )
    f_tt = lower(p_tt, 0.5).astype(BF)
    f_lt = p_l[:, top].astype(BF)
    f_ll = lower(p_l[:, low], 0.5).astype(BF)
    a_tt = dot2(inv_t_hi[top, :], inv_t_lo[top, :], jnp.concatenate([f_tt, f_lt], axis=0))
    a_tl = dot2(inv_t_hi[top, low], inv_t_lo[top, low], f_ll)
    a_l = dot2(
        inv_t_hi[low, low], inv_t_lo[low, low], jnp.concatenate([f_lt, f_ll], axis=1)
    )
    left = jnp.concatenate(
        [
            jnp.concatenate([a_tt, a_tl], axis=1).astype(BF),
            a_l.astype(BF),
        ],
        axis=0,
    )
    full[:, top] = dot2r(left, inv_hi[:, top], inv_lo[:, top])
    full[:, low] = dot2r(left[:, low], inv_hi[low, low], inv_lo[low, low])
    value = full[...]
    grad = 0.5 * (value + value.T)
    out[...] = grad
    twice[...] = 2.0 * grad
    own = pl.multiple_of(lax.axis_index("gr") * BLK, BLK)
    rows = twice[pl.ds(own, BLK), :].astype(BF)
    curvature = jnp.dot(rows, prior[...], preferred_element_type=F32)
    inter[...] = bar[...].astype(F32)
    prior_bar = jnp.concatenate(
        [inter[pl.ds(t, BLK, stride=2), :] for t in range(2)], axis=1
    )
    rest[...] = prior_bar - curvature


def final_kernel(rest, keep, recv, out, inter):
    value = rest[...] - (keep[...] + recv[...].astype(F32))
    for t in range(2):
        inter[pl.ds(t, BLK, stride=2), :] = value[:, t * BLK : (t + 1) * BLK]
    out[...] = inter[...].astype(BF)


def ring_order(n):
    return list(range(0, n, 2)) + list(range(n - 1, 0, -2))


def shard_of(offset, n):
    me = lax.axis_index("gc")
    half = lax.div(me, 2)
    pos = jnp.where(lax.rem(me, 2) == 0, half, n - 1 - half)
    at = lax.rem(pos - offset + 2 * n, n)
    return jnp.where(at < n // 2, 2 * at, 2 * (n - 1 - at) + 1)


def accumulate(grad, off, n, below, inter, acc, first):
    j = shard_of(off, n)
    view = below[:, j]
    rows = natural(view.reshape(view.shape[0] * view.shape[1], view.shape[2]), inter)
    part = row_product(grad[...], rows)
    if first:
        acc[...] = part
    else:
        acc[...] += part


def step_kernel(offsets, n, first, *refs):
    if first:
        own, *parts, inv, below, acc = refs[: len(offsets) + 4]
        grads, inter = refs[len(offsets) + 4 : -1], refs[-1]
        accumulate(own, 0, n, below, inter, acc, True)
    else:
        *parts, inv, below, before, acc = refs[: len(offsets) + 4]
        grads, inter = refs[len(offsets) + 4 : -1], refs[-1]
        acc[...] = before[...]
    inverse = inv[...].astype(BF)
    for off, part, grad in zip(offsets, parts, grads):
        grad[...] = jnp.dot(part[...], inverse, preferred_element_type=F32).astype(BF)
        accumulate(grad, off, n, below, inter, acc, False)


def last_kernel(offset, n, count, *refs):
    parts = refs[:count]
    inv, below, before, keep, send, grad, inter, acc = refs[count:]
    acc[...] = before[...]
    inverse = inv[...].astype(BF)
    at = 0
    for part in parts:
        grad[at : at + part.shape[0], :] = jnp.dot(
            part[...], inverse, preferred_element_type=F32
        ).astype(BF)
        at += part.shape[0]
    accumulate(grad, offset, n, below, inter, acc, False)
    core = my_core()
    for which in range(2):
        for y in range(2):
            piece = acc[(2 * y + which) * BLK : (2 * y + which + 1) * BLK, :]

            @pl.when(core == which)
            def _():
                keep[y] = piece

            @pl.when(core != which)
            def _():
                send[y] = piece.astype(BF)


def spread(prod, inter):
    for t in range(2):
        inter[pl.ds(t, prod.shape[0], stride=2), :] = prod[:, t * BLK : (t + 1) * BLK]


def below_kernel(offsets, n, *refs):
    grads = refs[: len(offsets)]
    p_own, p_other, bar, out, last, whole, done, inter, small = refs[len(offsets) :]
    done[...] = jnp.zeros_like(done)
    natural_prior(p_own, p_other, small, whole)
    for grad, off in zip(grads, offsets):
        j = shard_of(off, n)
        spread(jnp.dot(grad[...], whole[...], preferred_element_type=F32), inter)
        view = bar[:, j]
        old = view.reshape(view.shape[0] * view.shape[1], view.shape[2]).astype(F32)
        out[:, j] = (old - inter[...]).astype(BF).reshape(view.shape)
    rest = bar[:, shard_of(n // 2, n)]
    last[...] = rest.reshape(rest.shape[0] * rest.shape[1], rest.shape[2])


def below_last_kernel(n, early, grad, whole, bar, out, inter, block, sem):
    spread(jnp.dot(grad[...], whole[...], preferred_element_type=F32), inter)
    block[...] = (bar[...].astype(F32) - inter[...]).astype(BF).reshape(block.shape)
    copy = pltpu.make_async_copy(block, out.at[:, shard_of(n // 2, n)], sem)
    copy.start()
    copy.wait()


def in_hbm(value):
    return pltpu.with_memory_space_constraint(value, pltpu.HBM)


def tie(value, *after):
    return lax.optimization_barrier((value, *after))[0]


def xor_perm(n, bit):
    return [(i, i ^ bit) for i in range(n)]


def local_fast(
    below_factor,
    panel_factor,
    prior_factor,
    diag_factor,
    diag_inverse,
    below_adjoint,
    panel_adjoint,
    prior_adjoint,
    diag_adjoint,
    n_gr,
    n_gc,
):
    tiles, _, tile_rows, ct, _, cb = below_factor.shape
    own_rows, width = panel_factor.shape[2:]
    shard_rows = tiles * own_rows
    cols = ct * cb
    prior_local = prior_factor.shape[0]
    core = lambda v: lax.ppermute(v, "gr", xor_perm(n_gr, 1))
    ynb = lambda v: lax.ppermute(v, "gr", xor_perm(n_gr, 2))
    gcx = lambda v, bit: lax.ppermute(v, "gc", xor_perm(n_gc, bit))
    cyc = ring_order(n_gc)
    right = [(cyc[i], cyc[(i + 1) % n_gc]) for i in range(n_gc)]
    left = [(b, a) for a, b in right]

    bf_view = below_factor.reshape(tiles, n_gc, own_rows * ct, cb)
    ba_view = below_adjoint.reshape(tiles, n_gc, own_rows * ct, cb)
    pf_view = prior_factor.reshape(prior_local * ct, cb)
    pa_view = prior_adjoint.reshape(prior_local * ct, cb)

    n_blocks = len(lower_blocks(width // BLK))
    half_rows = n_blocks // 2 * BLK
    quarter = half_rows // 2
    adj2 = panel_adjoint.reshape(shard_rows, width)
    shard = ((shard_rows, width), BF)
    token = ((8, BLK), F32)

    def step_call(name, offs, parts, acc=None):
        return call(
            functools.partial(step_kernel, offs, n_gc, acc is None),
            [((width, cols), F32)] + [shard] * len(offs),
            [*parts, diag_inverse, bf_view] + ([] if acc is None else [acc]),
            scratch=[pltpu.VMEM((shard_rows * ct, cb), F32)],
            name=name,
        )

    grad, keep, send = call(
        grad_kernel,
        [
            ((shard_rows, width), BF),
            ((half_rows, BLK), F32),
            ((half_rows + prior_local * ct, BLK), BF),
        ],
        [
            in_hbm(v)
            for v in (adj2, panel_factor.reshape(shard_rows, width), diag_inverse, pf_view)
        ],
        scratch=[
            pltpu.VMEM((shard_rows, width), BF),
            pltpu.VMEM((shard_rows, width), BF),
            pltpu.VMEM((width, width), F32),
            pltpu.VMEM((shard_rows, width), BF),
            pltpu.SemaphoreType.DMA((5,)),
        ],
        name="panel_grad",
        specs=[ANYM] * 4,
        out_specs=[ANYM, VM, VM],
    )

    to_right = lambda v: lax.ppermute(v, "gc", right)
    to_left = lambda v: lax.ppermute(v, "gc", left)
    plus = lambda a, b: (a.astype(F32) + b.astype(F32)).astype(BF)
    y = my_y()
    env = {}
    done = {}

    def need(item):
        if item in done:
            return
        done[item] = True
        if item == "r1":
            env["r1"] = [to_right(adj2), to_left(adj2)]
        elif item in ("r2", "r3"):
            before = "r%d" % (int(item[1]) - 1)
            need(before)
            u, v = env[before]
            env[item] = [to_right(u), to_left(v)]
        elif item == "r4":
            need("r3")
            u, v = env["r3"]
            env[item] = [to_right(u[:CUT]), to_left(v[CUT:])] if SPLIT else [to_right(u)]
        elif item in ("s1", "s2", "s3"):
            k = int(item[1])
            need("r%d" % k)
            if k > 1:
                need("s%d" % (k - 1))
            lead = [grad] if k == 1 else []
            acc, *out = step_call(
                "step_%d" % k, [k, -k], [*lead, *env["r%d" % k]],
                None if k == 1 else env["s%d" % (k - 1)][0],
            )
            env[item], env["g%d" % k] = [acc], out
        elif item == "prep":
            *out, mark = call(
                prep_kernel,
                [((width, width), BF)] * 6 + [token],
                [diag_factor, diag_inverse],
                name="prep",
            )
            env["prepared"], env[item] = out, [mark]
        elif item == "pf":
            env[item] = [ynb(env["pair"])]
        elif item == "below":
            need("s3")
            need("pf")
            offsets = [0, 1, -1, 2, -2, 3, -3]
            grads = [grad, *env["g1"], *env["g2"], *env["g3"]]
            out, bar, whole, mark = call(
                functools.partial(below_kernel, offsets, n_gc),
                [(ba_view.shape, BF), ((shard_rows * ct, cb), BF), ((width, cols), BF), token],
                [*grads, env["pair"], *env["pf"], ba_view],
                scratch=[
                    pltpu.VMEM((shard_rows * ct, cb), F32),
                    pltpu.VMEM((prior_local * ct, cb), F32),
                ],
                name="below_early",
            )
            env["early"], env[item] = (out, bar, whole), [mark]
        elif item == "s4":
            need("r4")
            need("s3")
            keep_x, send_x, g4 = call(
                functools.partial(last_kernel, n_gc // 2, n_gc, len(env["r4"])),
                [((2, BLK, cols), F32), ((2, BLK, cols), BF), ((shard_rows, width), BF)],
                [*env["r4"], diag_inverse, bf_view, env["s3"][0]],
                scratch=[
                    pltpu.VMEM((shard_rows * ct, cb), F32),
                    pltpu.VMEM((width, cols), F32),
                ],
                name="step_four",
            )
            both_x = keep_x + core(send_x).astype(F32)
            env["mine_x"] = lax.dynamic_index_in_dim(both_x, y, 0, keepdims=False)
            other_x = lax.dynamic_index_in_dim(both_x, 1 - y, 0, keepdims=False).astype(BF)
            env["g4"], env[item] = g4, [other_x]

    def gate(point, value):
        items = [k for k, v in TIES.items() if v == point]
        for item in items:
            need(item)
        vals = [v for item in items for v in env[item]]
        if not vals:
            return value
        value, *vals = lax.optimization_barrier((value, *vals))
        for item in items:
            env[item] = [vals.pop(0) for _ in env[item]]
        return value

    got = gate("sum", core(gate("core", send)))
    both = (keep + got[:half_rows].astype(F32)).reshape(2, quarter, BLK)
    mine = lax.dynamic_index_in_dim(both, y, 0, keepdims=False)
    other = lax.dynamic_index_in_dim(both, 1 - y, 0, keepdims=False).astype(BF)
    env["pair"] = jnp.concatenate([pf_view, got[half_rows:]], axis=0)
    part = plus(mine, gate("ysum", ynb(gate("y", other))))
    for k, name in enumerate(("x", "z1", "z2")):
        part = gate(name, part)
        part = plus(part, gate(name + "sum", gcx(part, 1 << k)))
    part = gate("ag", part)
    part_y = gate("agsum", ynb(part))
    part_c = core(jnp.concatenate([part, part_y], axis=0))
    for item in ("prep", "below", "s4"):
        need(item)
    got_x = ynb(env["s4"][0])
    prepared = env["prepared"]
    below_early, last_bar, prior_whole = env["early"]
    marks = env["prep"] + env["below"]
    g4 = env["g4"]
    if LATE:
        part_c = tie(part_c, env["s4"][0])

    diag_gradient, rest = call(
        solve_kernel,
        [((width, width), F32), ((prior_local, cols), F32)],
        [part, part_y, part_c, prior_whole, pa_view, diag_adjoint, *prepared, *marks],
        scratch=[
            pltpu.VMEM((n_blocks * BLK, BLK), F32),
            pltpu.VMEM((width, width), F32),
            pltpu.VMEM((width, width), F32),
            pltpu.VMEM((prior_local * ct, cb), F32),
        ],
        flops=18 * width**3,
        nbytes=2**22,
        name="solve",
        specs=[VM] * 12 + [ANYM] * len(marks),
    )
    (below_new,) = call(
        functools.partial(below_last_kernel, n_gc),
        [(ba_view.shape, BF)],
        [below_early, g4, prior_whole, last_bar],
        scratch=[
            pltpu.VMEM((shard_rows * ct, cb), F32),
            pltpu.VMEM((tiles, own_rows * ct, cb), BF),
            pltpu.SemaphoreType.DMA(()),
        ],
        name="below_last",
        specs=[ANYM] + [VM] * 3,
        out_specs=[ANYM],
        alias={0: 0},
    )
    (prior_new,) = call(
        final_kernel,
        [(pa_view.shape, BF)],
        [rest, env["mine_x"], got_x],
        scratch=[pltpu.VMEM((prior_local * ct, cb), F32)],
        flops=10 * prior_local * cols,
        nbytes=2**18,
        name="prior_sum",
    )
    return (
        below_new.reshape(below_adjoint.shape),
        grad.reshape(panel_adjoint.shape),
        prior_new.reshape(prior_adjoint.shape),
        diag_gradient,
    )


def solution(mesh):
    n_gr, n_gc = mesh.shape["gr"], mesh.shape["gc"]

    def local(*args):
        below_factor, panel_factor, prior_factor = args[:3]
        fits = (
            n_gr == 4
            and n_gc == 8
            and panel_factor.shape[2] == 8
            and below_factor.shape[3] == 2
            and below_factor.shape[5] == BLK
            and prior_factor.shape[0] == BLK
        )
        if fits:
            return local_fast(*args, n_gr=n_gr, n_gc=n_gc)
        return local_any(*args)

    in_specs = (
        P(None, "gr", None, None, "gc", None),
        P(None, "gr", "gc", None),
        P("gr", None, "gc", None),
        P(),
        P(),
        P(None, "gr", None, None, "gc", None),
        P(None, "gr", "gc", None),
        P("gr", None, "gc", None),
        P(),
    )
    out_specs = (
        P(None, "gr", None, None, "gc", None),
        P(None, "gr", "gc", None),
        P("gr", None, "gc", None),
        P(),
    )
    return jax.shard_map(local, mesh=mesh, in_specs=in_specs, out_specs=out_specs, check_vma=False)
```

```python
import functools

import jax
import jax.numpy as jnp
from jax import lax
from jax.experimental import pallas as pl
from jax.experimental.pallas import tpu as pltpu
from jax.sharding import PartitionSpec as P

BF = jnp.bfloat16
F32 = jnp.float32
BLK = 128


def row_product(left_rows, right_rows):
    return lax.dot_general(
        left_rows, right_rows, (((0,), (0,)), ((), ())), preferred_element_type=F32
    )


def diag_solve(diag_factor, diag_inverse, diag_reduced):
    highest = lax.Precision.HIGHEST
    chol_proj = jnp.dot(diag_factor.T, diag_reduced, precision=highest)
    phi_lower = jnp.tril(chol_proj) - 0.5 * jnp.diag(jnp.diagonal(chol_proj))
    symmetric = 0.5 * (phi_lower + phi_lower.T)
    left_side = jnp.dot(diag_inverse.T, symmetric, precision=highest)
    return jnp.dot(left_side, diag_inverse, precision=highest)


def local_any(
    below_factor,
    panel_factor,
    prior_factor,
    diag_factor,
    diag_inverse,
    below_adjoint,
    panel_adjoint,
    prior_adjoint,
    diag_adjoint,
):
    tile_count = below_factor.shape[0]
    tile_rows = below_factor.shape[2]
    local_rows = tile_count * tile_rows
    local_cols = below_factor.shape[3] * below_factor.shape[5]
    own_rows = panel_factor.shape[2]
    width = panel_factor.shape[3]
    prior_local = prior_factor.shape[0]
    below_mat = below_factor.reshape(local_rows, local_cols)
    below_bar = below_adjoint.reshape(local_rows, local_cols)
    inverse_bf = diag_inverse.astype(BF)
    own_grad = jnp.dot(
        panel_adjoint.reshape(tile_count * own_rows, width),
        inverse_bf,
        preferred_element_type=F32,
    ).astype(BF)
    summed = lax.psum(
        row_product(own_grad, panel_factor.reshape(tile_count * own_rows, width)).astype(BF),
        ("gr", "gc"),
    ).astype(F32)
    panel_grad = own_grad.reshape(panel_adjoint.shape)
    grad_rows = lax.all_gather(panel_grad, "gc", axis=2, tiled=True).reshape(local_rows, width)
    diag_reduced = jnp.tril(diag_adjoint - summed)
    diag_gradient = diag_solve(diag_factor, diag_inverse, diag_reduced)
    prior_here = prior_factor.reshape(prior_local, local_cols)
    prior_whole = lax.all_gather(prior_here, "gr", axis=0, tiled=True)
    below_new = (
        below_bar.astype(F32) - jnp.dot(grad_rows, prior_whole, preferred_element_type=F32)
    ).astype(BF)
    crossing = lax.psum_scatter(
        row_product(grad_rows, below_mat).astype(BF), "gr", scatter_dimension=0, tiled=True
    ).astype(F32)
    twice_rows = lax.dynamic_slice_in_dim(
        2.0 * diag_gradient, lax.axis_index("gr") * prior_local, prior_local, 0
    ).astype(BF)
    curvature = jnp.dot(twice_rows, prior_whole, preferred_element_type=F32)
    prior_bar = prior_adjoint.reshape(prior_local, local_cols).astype(F32)
    prior_new = (prior_bar - crossing - curvature).astype(BF)
    return (
        below_new.reshape(below_adjoint.shape),
        panel_grad,
        prior_new.reshape(prior_adjoint.shape),
        diag_gradient,
    )


TIES = {'r1': 'sum', 'r2': 'xsum', 'r3': 'z1sum', 'r4': 'none', 's1': 'z1', 's2': 'z1sum', 's3': 'z2sum', 's4': 'none', 'pf': 'z1', 'prep': 'z1sum', 'below': 'ag'}
SPLIT, CUT, LATE, LIM = True, 112, True, 20 * 2**20
PAIRED = False
PREPC = 0
ONLY = (0, 2)
VM = pl.BlockSpec(memory_space=pltpu.VMEM)
ANYM = pl.BlockSpec(memory_space=pl.ANY)


def call(body, outs, ins, scratch=(), flops=0, nbytes=0, name=None, specs=None,
         out_specs=None, limit=LIM, alias=None):
    return pl.pallas_call(
        body,
        out_shape=[jax.ShapeDtypeStruct(s, d) for s, d in outs],
        in_specs=specs or [VM] * len(ins),
        out_specs=out_specs or [VM] * len(outs),
        scratch_shapes=list(scratch),
        compiler_params=pltpu.CompilerParams(vmem_limit_bytes=limit),
        cost_estimate=pl.CostEstimate(flops=flops, bytes_accessed=nbytes, transcendentals=0),
        name=name,
        input_output_aliases=alias or {},
    )(*ins)


def lower_blocks(count):
    return [(r, c) for r in range(count) for c in range(r + 1)]


def my_core():
    return lax.rem(lax.axis_index("gr"), 2)


def my_y():
    return lax.div(lax.axis_index("gr"), 2)


def grad_kernel(adj, fac, inv, prior, grad, keep, send, adj_v, fac_v, inv_v, grad_v, sems):
    half = keep.shape[0]
    pairs = [(adj, adj_v), (inv, inv_v), (fac, fac_v), (prior, send.at[half:, :])]
    copies = [
        pltpu.make_async_copy(src, dst, sems.at[k]) for k, (src, dst) in enumerate(pairs)
    ]
    for copy in copies:
        copy.start()
    copies[0].wait()
    copies[1].wait()
    grad_v[...] = jnp.dot(
        adj_v[...], inv_v[...].astype(BF), preferred_element_type=F32
    ).astype(BF)
    back = pltpu.make_async_copy(grad_v, grad, sems.at[4])
    back.start()
    copies[2].wait()
    blocks = lower_blocks(adj.shape[1] // BLK)
    core = my_core()
    whole = row_product(grad_v[...], fac_v[...])
    for at, (row, col) in enumerate(blocks):
        which, place = divmod(at * BLK, half)
        piece = whole[row * BLK : (row + 1) * BLK, col * BLK : (col + 1) * BLK]
        here = pl.ds(place, BLK)

        @pl.when(core == which)
        def _():
            keep[here, :] = piece

        @pl.when(core != which)
        def _():
            send[here, :] = piece.astype(BF)

    copies[3].wait()
    back.wait()


def prep_kernel(fac, inv, fac_t, inv_t, inv_bf, done):
    done[...] = jnp.zeros_like(done)
    fac_t[...] = fac[...].T.astype(BF)
    inv_t[...] = inv[...].T.astype(BF)
    inv_bf[...] = inv[...].astype(BF)


def product(a, b):
    return jnp.dot(a, b, preferred_element_type=F32)


def natural(view, scratch):
    rows = view.shape[0] // 2
    scratch[...] = view.astype(F32)
    return jnp.concatenate(
        [scratch[pl.ds(t, rows, stride=2), :] for t in range(2)], axis=1
    ).astype(BF)


def natural_prior(own, other, scratch, whole):
    rows = own.shape[0] // 2
    core, y = my_core(), my_y()
    for ref, where in ((own, y), (other, 1 - y)):
        for k in range(2):
            at = pl.multiple_of((2 * where + jnp.bitwise_xor(core, k)) * BLK, BLK)
            whole[pl.ds(at, BLK), :] = natural(ref[k * rows : (k + 1) * rows, :], scratch)


def solve_kernel(
    c_own, c_y, c_core, prior, bar, dadj,
    fac_t, inv_t, inv_bf, *others
):
    out, rest, cross, full, twice, inter = others[-6:]
    quarter = c_own.shape[0]
    core, y = my_core(), my_y()
    for where, off, ref in ((core, y, c_own[...]), (core, 1 - y, c_y[...]),
                            (1 - core, y, c_core[:quarter, :]),
                            (1 - core, 1 - y, c_core[quarter:, :])):
        at = pl.multiple_of((2 * where + off) * quarter, quarter)
        cross[pl.ds(at, quarter), :] = ref.astype(F32)
    size = dadj.shape[0]
    half = size // 2
    blocks = lower_blocks(size // BLK)
    top, low = slice(0, half), slice(half, size)
    r_at = lax.broadcasted_iota(jnp.int32, (half, half), 0)
    c_at = lax.broadcasted_iota(jnp.int32, (half, half), 1)

    def reduced(rows, cols):
        strips = []
        for row in range(rows.start // BLK, rows.stop // BLK):
            parts = []
            for col in range(cols.start // BLK, cols.stop // BLK):
                if col > row:
                    parts.append(jnp.zeros((BLK, BLK), F32))
                    continue
                at = blocks.index((row, col))
                here = dadj[row * BLK : (row + 1) * BLK, col * BLK : (col + 1) * BLK]
                parts.append(here - cross[at * BLK : (at + 1) * BLK, :])
            strips.append(jnp.concatenate(parts, axis=1))
        return jnp.concatenate(strips, axis=0)

    def lower(value, scale):
        zero = jnp.zeros_like(value)
        return jnp.where(r_at > c_at, value, jnp.where(r_at == c_at, scale * value, zero))

    d_tt = lower(reduced(top, top), 1.0).astype(BF)
    d_lt = reduced(low, top).astype(BF)
    d_ll = lower(reduced(low, low), 1.0).astype(BF)
    p_tt = product(fac_t[top, :], jnp.concatenate([d_tt, d_lt], axis=0))
    p_l = product(
        fac_t[low, low], jnp.concatenate([d_lt, d_ll], axis=1)
    )
    f_tt = lower(p_tt, 0.5).astype(BF)
    f_lt = p_l[:, top].astype(BF)
    f_ll = lower(p_l[:, low], 0.5).astype(BF)
    a_tt = product(inv_t[top, :], jnp.concatenate([f_tt, f_lt], axis=0))
    a_tl = product(inv_t[top, low], f_ll)
    a_l = product(
        inv_t[low, low], jnp.concatenate([f_lt, f_ll], axis=1)
    )
    left = jnp.concatenate(
        [
            jnp.concatenate([a_tt, a_tl], axis=1).astype(BF),
            a_l.astype(BF),
        ],
        axis=0,
    )
    full[:, top] = product(left, inv_bf[:, top])
    full[:, low] = product(left[:, low], inv_bf[low, low])
    value = full[...]
    grad = 0.5 * (value + value.T)
    out[...] = grad
    twice[...] = 2.0 * grad
    own = pl.multiple_of(lax.axis_index("gr") * BLK, BLK)
    rows = twice[pl.ds(own, BLK), :].astype(BF)
    curvature = jnp.dot(rows, prior[...], preferred_element_type=F32)
    inter[...] = bar[...].astype(F32)
    prior_bar = jnp.concatenate(
        [inter[pl.ds(t, BLK, stride=2), :] for t in range(2)], axis=1
    )
    rest[...] = prior_bar - curvature


def final_kernel(rest, keep, recv, out, inter):
    value = rest[...] - (keep[...] + recv[...].astype(F32))
    for t in range(2):
        inter[pl.ds(t, BLK, stride=2), :] = value[:, t * BLK : (t + 1) * BLK]
    out[...] = inter[...].astype(BF)


def ring_order(n):
    return list(range(0, n, 2)) + list(range(n - 1, 0, -2))


def shard_of(offset, n):
    me = lax.axis_index("gc")
    half = lax.div(me, 2)
    pos = jnp.where(lax.rem(me, 2) == 0, half, n - 1 - half)
    at = lax.rem(pos - offset + 2 * n, n)
    return jnp.where(at < n // 2, 2 * at, 2 * (n - 1 - at) + 1)


def accumulate(grad, off, n, below, inter, acc, first):
    j = shard_of(off, n)
    view = below[:, j]
    rows = natural(view.reshape(view.shape[0] * view.shape[1], view.shape[2]), inter)
    part = row_product(grad[...], rows)
    if first:
        acc[...] = part
    else:
        acc[...] += part


def step_kernel(offsets, n, first, *refs):
    grads, inter = refs[len(offsets) + 5 : -1], refs[-1]
    if first:
        own, *parts, inv, below, acc, done = refs[: len(offsets) + 5]
        accumulate(own, 0, n, below, inter, acc, True)
    else:
        *parts, inv, below, before, acc, done = refs[: len(offsets) + 5]
        acc[...] = before[...]
    done[...] = jnp.zeros_like(done)
    inverse = inv[...].astype(BF)
    for off, part, grad in zip(offsets, parts, grads):
        grad[...] = jnp.dot(part[...], inverse, preferred_element_type=F32).astype(BF)
        accumulate(grad, off, n, below, inter, acc, False)


def last_kernel(offset, n, count, *refs):
    parts = refs[:count]
    inv, below, before, keep, send, grad, inter, acc = refs[count:]
    acc[...] = before[...]
    inverse = inv[...].astype(BF)
    at = 0
    for part in parts:
        grad[at : at + part.shape[0], :] = jnp.dot(
            part[...], inverse, preferred_element_type=F32
        ).astype(BF)
        at += part.shape[0]
    accumulate(grad, offset, n, below, inter, acc, False)
    core = my_core()
    for which in range(2):
        for y in range(2):
            piece = acc[(2 * y + which) * BLK : (2 * y + which + 1) * BLK, :]

            @pl.when(core == which)
            def _():
                keep[y] = piece

            @pl.when(core != which)
            def _():
                send[y] = piece.astype(BF)


def spread(prod, inter):
    for t in range(2):
        inter[pl.ds(t, prod.shape[0], stride=2), :] = prod[:, t * BLK : (t + 1) * BLK]


def below_kernel(offsets, n, *refs):
    grads = refs[: len(offsets)]
    p_own, p_other, bar, out, last, whole, done, inter, small = refs[len(offsets) :]
    done[...] = jnp.zeros_like(done)
    natural_prior(p_own, p_other, small, whole)
    for grad, off in zip(grads, offsets):
        j = shard_of(off, n)
        spread(jnp.dot(grad[...], whole[...], preferred_element_type=F32), inter)
        view = bar[:, j]
        old = view.reshape(view.shape[0] * view.shape[1], view.shape[2]).astype(F32)
        out[:, j] = (old - inter[...]).astype(BF).reshape(view.shape)
    rest = bar[:, shard_of(n // 2, n)]
    last[...] = rest.reshape(rest.shape[0] * rest.shape[1], rest.shape[2])


def below_last_kernel(n, early, grad, whole, bar, out, inter, block, sem):
    spread(jnp.dot(grad[...], whole[...], preferred_element_type=F32), inter)
    block[...] = (bar[...].astype(F32) - inter[...]).astype(BF).reshape(block.shape)
    copy = pltpu.make_async_copy(block, out.at[:, shard_of(n // 2, n)], sem)
    copy.start()
    copy.wait()


def in_hbm(value):
    return pltpu.with_memory_space_constraint(value, pltpu.HBM)


def tie(value, *after):
    return lax.optimization_barrier((value, *after))[0]


def xor_perm(n, bit):
    return [(i, i ^ bit) for i in range(n)]


def local_fast(
    below_factor,
    panel_factor,
    prior_factor,
    diag_factor,
    diag_inverse,
    below_adjoint,
    panel_adjoint,
    prior_adjoint,
    diag_adjoint,
    n_gr,
    n_gc,
):
    tiles, _, tile_rows, ct, _, cb = below_factor.shape
    own_rows, width = panel_factor.shape[2:]
    shard_rows = tiles * own_rows
    cols = ct * cb
    prior_local = prior_factor.shape[0]
    core = lambda v: lax.ppermute(v, "gr", xor_perm(n_gr, 1))
    ynb = lambda v: lax.ppermute(v, "gr", xor_perm(n_gr, 2))
    gcx = lambda v, bit: lax.ppermute(v, "gc", xor_perm(n_gc, bit))
    cyc = ring_order(n_gc)
    right = [(cyc[i], cyc[(i + 1) % n_gc]) for i in range(n_gc)]
    left = [(b, a) for a, b in right]

    bf_view = below_factor.reshape(tiles, n_gc, own_rows * ct, cb)
    ba_view = below_adjoint.reshape(tiles, n_gc, own_rows * ct, cb)
    pf_view = prior_factor.reshape(prior_local * ct, cb)
    pa_view = prior_adjoint.reshape(prior_local * ct, cb)

    n_blocks = len(lower_blocks(width // BLK))
    half_rows = n_blocks // 2 * BLK
    quarter = half_rows // 2
    adj2 = panel_adjoint.reshape(shard_rows, width)
    shard = ((shard_rows, width), BF)
    token = ((8, BLK), F32)

    def step_call(name, offs, parts, acc=None):
        return call(
            functools.partial(step_kernel, offs, n_gc, acc is None),
            [((width, cols), F32), token] + [shard] * len(offs),
            [*parts, diag_inverse, bf_view] + ([] if acc is None else [acc]),
            scratch=[pltpu.VMEM((shard_rows * ct, cb), F32)],
            name=name,
        )

    grad, keep, send = call(
        grad_kernel,
        [
            ((shard_rows, width), BF),
            ((half_rows, BLK), F32),
            ((half_rows + prior_local * ct, BLK), BF),
        ],
        [
            in_hbm(v)
            for v in (adj2, panel_factor.reshape(shard_rows, width), diag_inverse, pf_view)
        ],
        scratch=[
            pltpu.VMEM((shard_rows, width), BF),
            pltpu.VMEM((shard_rows, width), BF),
            pltpu.VMEM((width, width), F32),
            pltpu.VMEM((shard_rows, width), BF),
            pltpu.SemaphoreType.DMA((5,)),
        ],
        name="panel_grad",
        specs=[ANYM] * 4,
        out_specs=[ANYM, VM, VM],
    )

    to_right = lambda v: lax.ppermute(v, "gc", right)
    to_left = lambda v: lax.ppermute(v, "gc", left)
    turn = [
        (g * n_gc + src, g * n_gc + dst)
        for g in range(n_gr)
        for src, dst in (right if g % 2 else left)
    ]
    plus = lambda a, b: (a.astype(F32) + b.astype(F32)).astype(BF)
    y = my_y()
    env = {}
    done = {}

    def need(item):
        if item in done:
            return
        done[item] = True
        if item == "r1":
            env["r1"] = [to_right(adj2), to_left(adj2)]
        elif item in ("r2", "r3"):
            before = "r%d" % (int(item[1]) - 1)
            need(before)
            step = "s%d" % (int(item[1]) - 1)
            if TIES[step] == item:
                need(step)
                *env[before], env[step][0] = lax.optimization_barrier(
                    (*env[before], env[step][0])
                )
            u, v = env[before]
            env[item] = [to_right(u), to_left(v)]
        elif item == "r4":
            need("r3")
            if TIES["s3"] == item:
                need("s3")
                *env["r3"], env["s3"][0] = lax.optimization_barrier(
                    (*env["r3"], env["s3"][0])
                )
            u, v = env["r3"]
            if SPLIT:
                env[item] = [to_right(u[:CUT]), to_left(v[CUT:])]
            else:
                env[item] = [lax.ppermute(jnp.where(my_core() == 1, u, v), ("gr", "gc"), turn)]
        elif item in ("s1", "s2", "s3"):
            k = int(item[1])
            need("r%d" % k)
            if k > 1:
                need("s%d" % (k - 1))
            lead = [grad] if k == 1 else []
            env["acc"], mark, *out = step_call(
                "step_%d" % k, [k, -k], [*lead, *env["r%d" % k]], env.get("acc")
            )
            env[item], env["g%d" % k] = [mark], out
        elif item == "prep":
            *out, mark = call(
                prep_kernel,
                [((width, width), BF)] * 3 + [token],
                [diag_factor, diag_inverse],
                name="prep",
                flops=PREPC,
            )
            env["prepared"], env[item] = out, [mark]
        elif item == "pf":
            if PAIRED:
                env[item] = [jnp.concatenate([env["pf_y"], core(env["pf_y"])], axis=0)]
            else:
                env[item] = [ynb(env["pair"])]
        elif item == "below":
            need("s3")
            need("pf")
            offsets = [0, 1, -1, 2, -2, 3, -3]
            grads = [grad, *env["g1"], *env["g2"], *env["g3"]]
            out, bar, whole, mark = call(
                functools.partial(below_kernel, offsets, n_gc),
                [(ba_view.shape, BF), ((shard_rows * ct, cb), BF), ((width, cols), BF), token],
                [*grads, env["pair"], *env["pf"], ba_view],
                scratch=[
                    pltpu.VMEM((shard_rows * ct, cb), F32),
                    pltpu.VMEM((prior_local * ct, cb), F32),
                ],
                name="below_early",
            )
            env["early"], env[item] = (out, bar, whole), [mark]
        elif item == "s4":
            need("r4")
            need("s3")
            keep_x, send_x, g4 = call(
                functools.partial(last_kernel, n_gc // 2, n_gc, len(env["r4"])),
                [((2, BLK, cols), F32), ((2, BLK, cols), BF), ((shard_rows, width), BF)],
                [*env["r4"], diag_inverse, bf_view, env["acc"]],
                scratch=[
                    pltpu.VMEM((shard_rows * ct, cb), F32),
                    pltpu.VMEM((width, cols), F32),
                ],
                name="step_four",
            )
            both_x = keep_x + core(send_x).astype(F32)
            env["mine_x"] = lax.dynamic_index_in_dim(both_x, y, 0, keepdims=False)
            other_x = lax.dynamic_index_in_dim(both_x, 1 - y, 0, keepdims=False).astype(BF)
            env["g4"], env[item] = g4, [other_x]

    def gate(point, value):
        items = [k for k, v in TIES.items() if v == point]
        for item in items:
            need(item)
        part_of = lambda item: slice(*ONLY) if item == "r1" else slice(None)
        vals = [v for item in items for v in env[item][part_of(item)]]
        if not vals:
            return value
        value, *vals = lax.optimization_barrier((value, *vals))
        for item in items:
            at = part_of(item)
            env[item][at] = [vals.pop(0) for _ in env[item][at]]
        return value

    got = gate("sum", core(gate("core", send)))
    both = (keep + got[:half_rows].astype(F32)).reshape(2, quarter, BLK)
    mine = lax.dynamic_index_in_dim(both, y, 0, keepdims=False)
    other = lax.dynamic_index_in_dim(both, 1 - y, 0, keepdims=False).astype(BF)
    env["pair"] = jnp.concatenate([pf_view, got[half_rows:]], axis=0)
    if PAIRED:
        arrived = ynb(gate("y", jnp.concatenate([other, pf_view], axis=0)))
        arrived = gate("ysum", arrived)
        env["pf_y"] = arrived[quarter:]
        part = plus(mine, arrived[:quarter])
    else:
        part = plus(mine, gate("ysum", ynb(gate("y", other))))
    for k, name in enumerate(("x", "z1", "z2")):
        part = gate(name, part)
        part = plus(part, gate(name + "sum", gcx(part, 1 << k)))
    part = gate("ag", part)
    part_y = gate("agsum", ynb(part))
    part_c = core(jnp.concatenate([part, part_y], axis=0))
    for item in ("prep", "below", "s4"):
        need(item)
    got_x = ynb(env["s4"][0])
    prepared = env["prepared"]
    below_early, last_bar, prior_whole = env["early"]
    marks = env["prep"] + env["below"] + env["s1"] + env["s2"] + env["s3"]
    g4 = env["g4"]
    if LATE:
        part_c = tie(part_c, env["s4"][0])

    diag_gradient, rest = call(
        solve_kernel,
        [((width, width), F32), ((prior_local, cols), F32)],
        [part, part_y, part_c, prior_whole, pa_view, diag_adjoint, *prepared, *marks],
        scratch=[
            pltpu.VMEM((n_blocks * BLK, BLK), F32),
            pltpu.VMEM((width, width), F32),
            pltpu.VMEM((width, width), F32),
            pltpu.VMEM((prior_local * ct, cb), F32),
        ],
        flops=18 * width**3,
        nbytes=2**22,
        name="solve",
        specs=[VM] * 9 + [ANYM] * len(marks),
    )
    (below_new,) = call(
        functools.partial(below_last_kernel, n_gc),
        [(ba_view.shape, BF)],
        [below_early, g4, prior_whole, last_bar],
        scratch=[
            pltpu.VMEM((shard_rows * ct, cb), F32),
            pltpu.VMEM((tiles, own_rows * ct, cb), BF),
            pltpu.SemaphoreType.DMA(()),
        ],
        name="below_last",
        specs=[ANYM] + [VM] * 3,
        out_specs=[ANYM],
        alias={0: 0},
    )
    (prior_new,) = call(
        final_kernel,
        [(pa_view.shape, BF)],
        [rest, env["mine_x"], got_x],
        scratch=[pltpu.VMEM((prior_local * ct, cb), F32)],
        flops=10 * prior_local * cols,
        nbytes=2**18,
        name="prior_sum",
    )
    return (
        below_new.reshape(below_adjoint.shape),
        grad.reshape(panel_adjoint.shape),
        prior_new.reshape(prior_adjoint.shape),
        diag_gradient,
    )


def solution(mesh):
    n_gr, n_gc = mesh.shape["gr"], mesh.shape["gc"]

    def local(*args):
        below_factor, panel_factor, prior_factor = args[:3]
        fits = (
            n_gr == 4
            and n_gc == 8
            and panel_factor.shape[2] == 8
            and below_factor.shape[3] == 2
            and below_factor.shape[5] == BLK
            and prior_factor.shape[0] == BLK
        )
        if fits:
            return local_fast(*args, n_gr=n_gr, n_gc=n_gc)
        return local_any(*args)

    in_specs = (
        P(None, "gr", None, None, "gc", None),
        P(None, "gr", "gc", None),
        P("gr", None, "gc", None),
        P(),
        P(),
        P(None, "gr", None, None, "gc", None),
        P(None, "gr", "gc", None),
        P("gr", None, "gc", None),
        P(),
    )
    out_specs = (
        P(None, "gr", None, None, "gc", None),
        P(None, "gr", "gc", None),
        P("gr", None, "gc", None),
        P(),
    )
    return jax.shard_map(local, mesh=mesh, in_specs=in_specs, out_specs=out_specs, check_vma=False)
```
